32 devices in a mesh: img: 8 (over y, x, core), pose: 4 (over z).
Axes of the slice: x: 2, y: 2, z: 4, core: 2. Of those that a mesh axis runs over, the one named last changes fastest.
Arguments:
- images: bfloat16 [1024, 8192], P('img'), may hold values from -240 to 240
- shift_phase: float32 [8, 4096], replicated, may hold values from -3.140625 to 3.140625
- noise_weight: float32 [8192], replicated, may hold values from 0.005 to 0.05
- refs: bfloat16 [1536, 8192], P('pose', 'img'), may hold values from -6 to 6
- routing: int32 [49152, 1], P(('pose', 'img')), may hold values from 0 to 31; in each aligned block of 1536 rows (0 to 1535, 1536 to 3071, ...) at most 96 rows name the same one
- stencil: int32 [49152], P(('pose', 'img')), may hold values from 0 to 7
- interp: bfloat16 [32, 8, 256, 512], P(('img', 'pose')), may hold values from -48 to 48
Outputs:
- volume: float32 [32, 512], P(('img', 'pose'))
- evidence: float32 [1024], P('img')
The draws below stay inside these ranges and needn't reach their ends.
Inputs may be any that keep to these rules, and one draw needn't show every extreme that they name: `routing`: among the rows of one device no brick is named more than 96 times, a bound that some block reaches there.
All inputs are finite; a program needn't handle non-finite values.
Results may differ from the reference program's by a relative error of at most 0.0052.
Values may be sent and summed in bfloat16 or wider, within the bound.
A program may use at most 192 MiB of HBM per device.

```python
import math
import jax
import jax.numpy as jnp
import numpy as np
from jax import lax

PIX = 4096
TRANS = 8
BLOCK = 128
STENCILS = 8
CELLS = 512
IMGS = 1024
POSES = 1536
NBLK = 32
BRICKS = 32
CAP = 96
DEVICES = 32


def draw_images(key, part):
    first_key = jax.random.fold_in(jax.random.fold_in(key, 11), 0)
    values = jnp.clip(jax.random.normal(first_key, (IMGS, 2 * PIX), jnp.float32), -6.0, 6.0)
    return values.astype(jnp.bfloat16)


def draw_refs(key, part):
    first_key = jax.random.fold_in(jax.random.fold_in(key, 23), 0)
    values = jnp.clip(jax.random.normal(first_key, (POSES, 2 * PIX), jnp.float32), -6.0, 6.0)
    return values.astype(jnp.bfloat16)


def with_ends(entries, stream_key, least, high):
    spot = [jax.random.randint(jax.random.fold_in(stream_key, axis), (), 0, length) for axis, length in enumerate(entries.shape)]
    widest = entries.shape.index(max(entries.shape))
    next_to = spot[:widest] + [(spot[widest] + 1) % entries.shape[widest]] + spot[widest + 1:]
    return entries.at[tuple(spot)].set(least).at[tuple(next_to)].set(high)


def levels(key, dims, pieces, least, largest):
    def one(axis_at, parts):
        heights = jax.random.uniform(jax.random.fold_in(jax.random.fold_in(key, 6), axis_at), (parts,), jnp.float32, least / len(pieces), largest / len(pieces))
        return jnp.repeat(jnp.exp(heights), dims[axis_at] // parts).reshape((-1,) + (1,) * (len(dims) - axis_at - 1))

    loudness = one(*pieces[0])
    for cut in pieces[1:]:
        loudness = loudness * one(*cut)
    return loudness


def routed_block(own_key, own, number, rows, amount, top, reach, lean):
    sequence = jax.random.permutation(own_key, amount)
    heavy_load, ordinary = portions_of(amount, rows * top, reach, lean, True), portions_of(amount, rows * top, reach, lean, False)
    places = jnp.arange(amount)

    def named(sizes, rotation):
        used = int((sizes > 0).sum())
        fixed = max(1, used // 4)
        passed = fixed + (places - fixed + rotation * (used - fixed)) % max(1, amount - fixed)
        return jnp.zeros((amount,), jnp.int32).at[sequence[jnp.where(places < fixed, places, passed)]].set(jnp.asarray(sizes, jnp.int32))

    sizes = jnp.where(number % 4 == 0, named(heavy_load, number // 4), named(ordinary, number - number // 4 - 1))
    mixed = jax.random.permutation(jax.random.fold_in(own, 3), amount)
    donor, taker = mixed[0:amount // 2 * 2:2], mixed[1:amount // 2 * 2:2]
    room = jnp.minimum(sizes[donor] - 1, reach - sizes[taker]) // 2
    room = jnp.where((donor == sequence[0]) | (taker == sequence[0]) | (sizes[taker] == 0), 0, jnp.maximum(room, 0))
    passed = jax.random.randint(jax.random.fold_in(own, 4), (amount // 2,), 0, 1 << 20) % (room + 1)
    sizes = sizes.at[donor].add(-passed).at[taker].add(passed)
    members = jnp.searchsorted(jnp.cumsum(sizes), jnp.arange(rows * top), side="right").astype(jnp.int32)
    grid = members.reshape(top, rows).T
    grid = grid[jax.random.permutation(jax.random.fold_in(own, 1), rows)]
    rotation = jax.random.randint(jax.random.fold_in(own, 2), (rows, 1), 0, top)
    return jnp.take_along_axis(grid, (jnp.arange(top)[None, :] + rotation) % top, axis=1)


def portions_of(amount, total, most, slope, full):
    loads = [(1 << 20) // math.isqrt(standing ** slope) + 1 for standing in range(1, amount + 1)]
    largest = most if full else min(most, max(-(-total // amount), total * loads[0] // sum(loads)))
    least = 1 if total - largest >= amount - 1 else 0
    given, rest = [largest] + [least] * (amount - 1), total - largest - least * (amount - 1)
    while rest > 0:
        candidates = [i for i in range(1, amount) if given[i] < largest] or [i for i in range(1, amount) if given[i] < most]
        whole, budget = sum([loads[i] for i in candidates]), rest
        for i in candidates:
            more = min(most - given[i], max(1, budget * loads[i] // whole), rest)
            given[i] = given[i] + more
            rest = rest - more
    return np.array(given)


def scatter_about(key, shape, spread, bound, cuts=(), held_as=jnp.bfloat16):
    array = spread * jax.random.normal(key, shape, jnp.float32)
    if cuts:
        array = array * levels(key, shape, cuts, -0.22, 0.18)
    return jnp.clip(array, -bound, bound).astype(held_as)


def setup_inputs(seed: int = 0) -> dict:
    streams_of = jax.random.split(jax.random.key(seed), 8)
    images = draw_images(jax.random.fold_in(streams_of[7], 71), 0)
    shift_phase = jnp.clip(jax.random.uniform(streams_of[1], (TRANS, PIX), jnp.float32, -3.140625, 3.140625), -3.140625, 3.140625)
    noise_weight = jnp.clip(jnp.exp(jax.random.uniform(streams_of[2], (2 * PIX,), jnp.float32, math.log(0.005), math.log(0.05))), 0.005, 0.05)
    refs = draw_refs(jax.random.fold_in(streams_of[7], 71), 0)
    routing_keys = jax.random.split(jax.random.fold_in(streams_of[4], 1), (POSES * NBLK) // (POSES * NBLK // DEVICES))
    routing_turns = jax.random.permutation(jax.random.fold_in(streams_of[4], 3), (POSES * NBLK) // (POSES * NBLK // DEVICES))
    routing = jax.vmap(lambda own, number: routed_block(jax.random.fold_in(streams_of[4], 2), own, number, POSES * NBLK // DEVICES, BRICKS, 1, CAP, 2))(routing_keys, routing_turns).reshape((POSES * NBLK, 1))
    stencil = with_ends(jax.random.randint(streams_of[5], (POSES * NBLK,), 0, STENCILS), jax.random.fold_in(streams_of[5], 1), 0, STENCILS - 1).astype(jnp.int32)
    interp = scatter_about(streams_of[6], (BRICKS, STENCILS, 2 * BLOCK, CELLS), 8.0, 48.0, ((0, 32),))
    return dict(images=images, shift_phase=shift_phase, noise_weight=noise_weight, refs=refs, routing=routing, stencil=stencil, interp=interp)


def translated(images, shift_phase, noise_weight):
    count = images.shape[0]
    blocks = images.astype(jnp.float32).reshape(count, 1, PIX // BLOCK, 2, BLOCK)
    real_part = blocks[:, :, :, 0, :]
    imag_part = blocks[:, :, :, 1, :]
    angles = shift_phase.reshape(1, TRANS, PIX // BLOCK, BLOCK)
    cosine = jnp.cos(angles)
    sine = jnp.sin(angles)
    new_real = real_part * cosine + imag_part * sine
    new_imag = imag_part * cosine - real_part * sine
    stacked = jnp.stack([new_real, new_imag], axis=3).reshape(count * TRANS, 2 * PIX)
    return (stacked * noise_weight[None, :]).astype(jnp.bfloat16)

def brick_volume(pair):
    gathered_row, matrices = pair
    flat = matrices.reshape(STENCILS * 2 * BLOCK, CELLS)
    return jnp.dot(gathered_row[None, :], flat, preferred_element_type=jnp.float32)[0]

def reference(images, shift_phase, noise_weight, refs, routing, stencil, interp):
    weighted = translated(images, shift_phase, noise_weight)
    refs_wide = refs.astype(jnp.float32)
    half_norm = 0.5 * lax.optimization_barrier(jnp.sum(refs_wide * refs_wide * noise_weight[None, :], axis=1))
    scores = lax.dot_general(weighted, refs, (((1,), (1,)), ((), ())), preferred_element_type=jnp.float32)
    scores = scores - half_norm[None, :]
    grouped = scores.reshape(IMGS, TRANS * POSES)
    peak = lax.optimization_barrier(jnp.max(grouped, axis=1))
    expo = jnp.exp(grouped - peak[:, None])
    total = lax.optimization_barrier(jnp.sum(expo, axis=1))
    evidence = peak + jnp.log(total)
    posterior = (expo / total[:, None]).astype(jnp.bfloat16).reshape(IMGS * TRANS, POSES)
    accum = lax.dot_general(posterior, weighted, (((0,), (0,)), ((), ())), preferred_element_type=jnp.float32)
    block_rows = accum.astype(jnp.bfloat16).reshape(POSES * NBLK, 2 * BLOCK)
    target = routing[:, 0].astype(jnp.int32)
    segment_ids = (target * STENCILS + stencil).astype(jnp.int32)
    gathered = jax.ops.segment_sum(block_rows.astype(jnp.float32), segment_ids, num_segments=BRICKS * STENCILS)
    gathered = gathered.astype(jnp.bfloat16).reshape(BRICKS, STENCILS * 2 * BLOCK)
    summed = lax.map(brick_volume, (gathered, interp))
    counts = jax.ops.segment_sum(jnp.ones((POSES * NBLK,), jnp.float32), target, num_segments=BRICKS)
    volume = summed * lax.rsqrt(1.0 + counts)[:, None]
    return (volume, evidence)
```

```python
import functools

import jax
import jax.numpy as jnp
from jax import lax
from jax.experimental import pallas as pl
from jax.experimental.pallas import tpu as pltpu
from jax.sharding import PartitionSpec as P

MESH = pl.DeviceIdType.MESH
F32 = jnp.float32
BF16 = jnp.bfloat16
LANES = 128


def remote(src, dst, send_sem, recv_sem, device):
    return pltpu.make_async_remote_copy(
        src_ref=src,
        dst_ref=dst,
        send_sem=send_sem,
        recv_sem=recv_sem,
        device_id=device,
        device_id_type=MESH,
    )


def kernel(
    n,
    pn,
    trans,
    images,
    table,
    noise,
    refs,
    seg,
    interp,
    volume,
    evidence,
    cols,
    weighted,
    scores,
    post,
    seg_all,
    seg_t,
    norm_acc,
    stats,
    part,
    part16,
    rows_in,
    message,
    bricks_in,
    matrices,
    gather_send,
    gather_recv,
    seg_send,
    seg_recv,
    stat_send,
    stat_recv,
    rows_send,
    rows_recv,
    brick_send,
    brick_recv,
    local_sem,
):
    me = lax.axis_index("img")
    mine = lax.axis_index("pose")
    core = me % 2
    chip = me // 2
    chips = n // 2
    partner = chip * 2 + 1 - core
    count, width = images.shape
    poses, depth = refs.shape
    share = seg.shape[0]
    block2 = 2 * LANES
    nblk = width // block2
    stencils = interp.shape[0]

    fetch = pltpu.make_async_copy(interp, matrices, local_sem)
    fetch.start()

    barrier = pltpu.get_barrier_semaphore()
    for d in range(1, n):
        pl.semaphore_signal(
            barrier, inc=1, device_id={"img": (me + d) % n}, device_id_type=MESH
        )
    for d in range(1, pn):
        pl.semaphore_signal(
            barrier, inc=1, device_id={"pose": (mine + d) % pn}, device_id_type=MESH
        )
    pl.semaphore_wait(barrier, n - 1 + pn - 1)

    sends = []
    for d in range(1, chips):
        target = ((chip + d) % chips) * 2 + core
        copy = remote(
            refs, cols.at[me], gather_send.at[d - 1], gather_recv.at[me], {"img": target}
        )
        copy.start()
        sends.append(copy)
    copy = remote(
        refs, cols.at[me], gather_send.at[chips - 1], gather_recv.at[me], {"img": partner}
    )
    copy.start()
    sends.append(copy)
    for d in range(1, n):
        copy = remote(
            seg,
            seg_all.at[pl.ds(pl.multiple_of(me * share, 8), share)],
            seg_send.at[d - 1],
            seg_recv.at[me],
            {"img": (me + d) % n},
        )
        copy.start()
        sends.append(copy)
    seg_all[pl.ds(pl.multiple_of(me * share, 8), share), :] = seg[...]

    @pl.loop(0, nblk)
    def _(b):
        at = pl.multiple_of(b * block2, block2)
        half = pl.multiple_of(b * LANES, LANES)
        re = images[:, pl.ds(at, LANES)].astype(F32)
        im = images[:, pl.ds(at + LANES, LANES)].astype(F32)
        for t in range(trans):
            co_r = table[t : t + 1, pl.ds(half, LANES)]
            si_r = table[trans + t : trans + t + 1, pl.ds(half, LANES)]
            co_i = table[2 * trans + t : 2 * trans + t + 1, pl.ds(half, LANES)]
            si_i = table[3 * trans + t : 3 * trans + t + 1, pl.ds(half, LANES)]
            rows = pl.ds(t * count, count)
            weighted[rows, pl.ds(at, LANES)] = (re * co_r + im * si_r).astype(BF16)
            weighted[rows, pl.ds(at + LANES, LANES)] = (im * co_i - re * si_i).astype(BF16)

    norm_acc[...] = jnp.zeros_like(norm_acc)
    total_rows = trans * count
    tile = min(512, total_rows)

    def multiply(block, src, first):
        start = pl.multiple_of(src * depth, LANES)

        @pl.loop(0, total_rows // tile)
        def _(r):
            rows = pl.ds(pl.multiple_of(r * tile, tile), tile)
            product = lax.dot_general(
                weighted[rows, pl.ds(start, depth)],
                block[...],
                (((1,), (1,)), ((), ())),
                preferred_element_type=F32,
            )
            if first:
                scores[rows, :] = product
            else:
                scores[rows, :] += product

        for g in range(depth // LANES):
            values = block[:, g * LANES : (g + 1) * LANES].astype(F32)
            lane_noise = noise[:, pl.ds(pl.multiple_of(start + g * LANES, LANES), LANES)]
            norm_acc[...] += values * values * lane_noise

    for d in range(chips):
        other = (chip + chips - d) % chips
        near = other * 2 + core
        far = other * 2 + 1 - core
        if d == 0:
            multiply(refs, near, True)
        else:
            remote(
                refs, cols.at[near], gather_send.at[0], gather_recv.at[near], {"img": partner}
            ).wait_recv()
            copy = remote(
                cols.at[near],
                cols.at[near],
                gather_send.at[chips - 1 + d],
                gather_recv.at[near],
                {"img": partner},
            )
            copy.start()
            sends.append(copy)
            multiply(cols.at[near], near, False)
        remote(
            refs, cols.at[far], gather_send.at[0], gather_recv.at[far], {"img": partner}
        ).wait_recv()
        multiply(cols.at[far], far, False)

    norm = 0.5 * jnp.sum(norm_acc[...].T, axis=0, keepdims=True)
    peak_wide = None
    for t in range(trans):
        rows = pl.ds(t * count, count)
        value = scores[rows, :] - norm
        scores[rows, :] = value
        peak_wide = value if peak_wide is None else jnp.maximum(peak_wide, value)
    local_peak = jnp.max(peak_wide, axis=1, keepdims=True)
    sum_wide = jnp.zeros((count, poses), F32)
    for t in range(trans):
        rows = pl.ds(t * count, count)
        value = jnp.exp(scores[rows, :] - local_peak)
        scores[rows, :] = value
        sum_wide += value
    local_sum = jnp.sum(sum_wide, axis=1, keepdims=True)
    lane = lax.broadcasted_iota(jnp.int32, (count, LANES), 1)
    both = jnp.where(lane == 0, local_peak, jnp.where(lane == 1, local_sum, 0.0))
    stats[mine] = both.T[0:8, :]
    for d in range(1, pn):
        copy = remote(
            stats.at[mine],
            stats.at[mine],
            stat_send.at[d - 1],
            stat_recv.at[mine],
            {"pose": (mine + d) % pn},
        )
        copy.start()
        sends.append(copy)

    for d in range(1, n):
        src = (me + n - d) % n
        remote(
            seg,
            seg_all.at[pl.ds(pl.multiple_of(src * share, 8), share)],
            seg_send.at[0],
            seg_recv.at[src],
            {"img": partner},
        ).wait_recv()
    seg_t[...] = seg_all[...].T

    for d in range(1, pn):
        src = (mine + pn - d) % pn
        remote(
            stats.at[src], stats.at[src], stat_send.at[0], stat_recv.at[src],
            {"pose": (mine + 1) % pn},
        ).wait_recv()
    peak = stats[0][0:1, :]
    for p in range(1, pn):
        peak = jnp.maximum(peak, stats[p][0:1, :])
    total = jnp.zeros((1, count), F32)
    for p in range(pn):
        total += stats[p][1:2, :] * jnp.exp(stats[p][0:1, :] - peak)
    evidence[...] = peak + jnp.log(total)
    factor = jnp.exp(stats[mine][0:1, :] - peak) / total
    factor = jnp.broadcast_to(factor, (count, count)).T[:, 0:1]
    for t in range(trans):
        rows = pl.ds(t * count, count)
        value = scores[rows, :] * factor
        post[:, t * count : (t + 1) * count] = value.T.astype(BF16)

    segments = part.shape[0]
    part[...] = jnp.zeros_like(part)

    @pl.loop(0, nblk)
    def _(b):
        at = pl.multiple_of(b * block2, block2)
        sums = jnp.dot(post[...], weighted[:, pl.ds(at, block2)], preferred_element_type=F32)
        names = lax.broadcasted_iota(jnp.int32, (segments, poses), 0).astype(F32)
        chosen = jnp.where(names == seg_t[pl.ds(b, 1), :], 1.0, 0.0).astype(BF16)
        part[...] += jnp.dot(chosen, sums.astype(BF16), preferred_element_type=F32)

    part16[...] = part[...].astype(BF16)
    group = pn * stencils
    for d in range(1, n):
        target = (me + d) % n
        copy = remote(
            part16.at[pl.ds(pl.multiple_of(target * group, 16), group)],
            rows_in.at[me],
            rows_send.at[d - 1],
            rows_recv.at[me],
            {"img": target},
        )
        copy.start()
        sends.append(copy)
    summed = part[pl.ds(pl.multiple_of(me * group, 16), group), :]
    message[...] = jnp.zeros_like(message)
    for p in range(pn):
        low = ((me * pn + p) * stencils).astype(F32)
        named = seg_all[...]
        inside = jnp.where((named >= low) & (named < low + stencils), 1.0, 0.0)
        message[p, stencils : stencils + 1, 0:LANES] = jnp.sum(inside, axis=0, keepdims=True)
    for d in range(1, n):
        src = (me + n - d) % n
        remote(
            rows_in.at[src], rows_in.at[src], rows_send.at[0], rows_recv.at[src],
            {"img": partner},
        ).wait_recv()
        summed += rows_in[src].astype(F32)
    for p in range(pn):
        message[p, 0:stencils, :] = summed[p * stencils : (p + 1) * stencils, :]
    for d in range(1, pn):
        target = (mine + d) % pn
        copy = remote(
            message.at[target],
            bricks_in.at[mine],
            brick_send.at[d - 1],
            brick_recv.at[mine],
            {"pose": target},
        )
        copy.start()
        sends.append(copy)
    brick = message[mine]
    fetch.wait()
    for d in range(1, pn):
        src = (mine + pn - d) % pn
        remote(
            bricks_in.at[src], bricks_in.at[src], brick_send.at[0], brick_recv.at[src],
            {"pose": (mine + 1) % pn},
        ).wait_recv()
        brick += bricks_in[src]
    gathered = brick[0:stencils, :].astype(BF16).astype(F32)
    received = jnp.sum(brick[stencils : 2 * stencils, :])
    row = lax.broadcasted_iota(jnp.int32, gathered.shape, 0)
    out = jnp.zeros((stencils, volume.shape[1]), F32)
    for s in range(stencils):
        out += jnp.dot(
            jnp.where(row == s, gathered, 0.0).astype(BF16),
            matrices[s],
            preferred_element_type=F32,
        )
    scale = lax.rsqrt(jnp.full((1, volume.shape[1]), 1.0, F32) + received)
    volume[...] = jnp.sum(out, axis=0, keepdims=True) * scale
    for copy in sends:
        copy.wait_send()


def body(images, shift_phase, noise_weight, refs, routing, stencil, interp):
    n = lax.axis_size("img")
    pn = lax.axis_size("pose")
    count, width = images.shape
    trans, pixels = shift_phase.shape
    poses, depth = refs.shape
    stencils = interp.shape[1]
    segments = n * pn * stencils
    nblk = pixels // LANES
    share = poses // n
    cosine = jnp.cos(shift_phase)
    sine = jnp.sin(shift_phase)
    split = noise_weight.reshape(nblk, 2, LANES)
    real_noise = split[:, 0, :].reshape(1, pixels)
    imag_noise = split[:, 1, :].reshape(1, pixels)
    table = jnp.concatenate(
        [cosine * real_noise, sine * real_noise, cosine * imag_noise, sine * imag_noise], axis=0
    )
    seg = (routing[:, 0] * stencils + stencil).astype(F32).reshape(share, nblk)
    seg = jnp.pad(seg, ((0, 0), (0, LANES - nblk)), constant_values=-1.0)
    vmem = pl.BlockSpec(memory_space=pltpu.VMEM)
    dma = pltpu.SemaphoreType.DMA
    flops = 4 * trans * count * width * poses
    volume, evidence = pl.pallas_call(
        functools.partial(kernel, n, pn, trans),
        out_shape=(
            jax.ShapeDtypeStruct((1, interp.shape[3]), F32),
            jax.ShapeDtypeStruct((1, count), F32),
        ),
        in_specs=[vmem] * 5 + [pl.BlockSpec(memory_space=pl.ANY)],
        out_specs=(vmem, vmem),
        scratch_shapes=[
            pltpu.VMEM((n, poses, depth), BF16),
            pltpu.VMEM((trans * count, width), BF16),
            pltpu.VMEM((trans * count, poses), F32),
            pltpu.VMEM((poses, trans * count), BF16),
            pltpu.VMEM((poses, LANES), F32),
            pltpu.VMEM((LANES, poses), F32),
            pltpu.VMEM((poses, LANES), F32),
            pltpu.VMEM((pn, 8, count), F32),
            pltpu.VMEM((segments, 2 * LANES), F32),
            pltpu.VMEM((segments, 2 * LANES), BF16),
            pltpu.VMEM((n, pn * stencils, 2 * LANES), BF16),
            pltpu.VMEM((pn, 2 * stencils, 2 * LANES), F32),
            pltpu.VMEM((pn, 2 * stencils, 2 * LANES), F32),
            pltpu.VMEM(interp.shape[1:], BF16),
            dma((n,)),
            dma((n,)),
            dma((n,)),
            dma((n,)),
            dma((pn,)),
            dma((pn,)),
            dma((n,)),
            dma((n,)),
            dma((pn,)),
            dma((pn,)),
            dma,
        ],
        compiler_params=pltpu.CompilerParams(
            collective_id=0, has_side_effects=True, vmem_limit_bytes=56 * 1024 * 1024
        ),
        cost_estimate=pl.CostEstimate(
            flops=flops, bytes_accessed=8 * 1024 * 1024, transcendentals=trans * count * poses
        ),
    )(images, table, noise_weight.reshape(1, width), refs, seg, interp[0])
    return (volume, evidence.reshape(count))


def solution(mesh):
    return jax.shard_map(
        body,
        mesh=mesh,
        in_specs=(
            P("img", None),
            P(),
            P(),
            P("pose", "img"),
            P(("pose", "img"), None),
            P(("pose", "img")),
            P(("img", "pose"), None, None, None),
        ),
        out_specs=(P(("img", "pose"), None), P("img")),
        check_vma=False,
    )
```

```python
import functools

import jax
import jax.numpy as jnp
from jax import lax
from jax.experimental import pallas as pl
from jax.experimental.pallas import tpu as pltpu
from jax.sharding import PartitionSpec as P

MESH = pl.DeviceIdType.MESH
F32 = jnp.float32
BF16 = jnp.bfloat16
LANES = 128


def remote(src, dst, send_sem, recv_sem, device):
    return pltpu.make_async_remote_copy(
        src_ref=src,
        dst_ref=dst,
        send_sem=send_sem,
        recv_sem=recv_sem,
        device_id=device,
        device_id_type=MESH,
    )


def kernel(
    n,
    pn,
    images,
    phase,
    noise,
    refs,
    seg,
    interp,
    volume,
    evidence,
    cols,
    weighted,
    scores,
    post,
    seg_all,
    seg_t,
    norms,
    stats,
    part,
    part16,
    rows_in,
    message,
    bricks_in,
    matrices,
    own_send,
    pass_send,
    diag_send,
    gather_recv,
    seg_send,
    seg_recv,
    norm_send,
    norm_recv,
    stat_send,
    stat_recv,
    rows_send,
    rows_recv,
    brick_send,
    brick_recv,
    local_sem,
):
    me = lax.axis_index("img")
    mine = lax.axis_index("pose")
    core = me % 2
    chip = me // 2
    chips = n // 2
    partner = chip * 2 + 1 - core
    count, width = images.shape
    trans = phase.shape[0]
    poses, depth = refs.shape
    piece = depth // 2
    share = seg.shape[0]
    block2 = 2 * LANES
    nblk = width // block2
    stencils = interp.shape[0]
    sends = []

    def send(src, dst, send_sem, recv_sem, device):
        copy = remote(src, dst, send_sem, recv_sem, device)
        copy.start()
        sends.append(copy)

    fetch = pltpu.make_async_copy(interp, matrices, local_sem)
    fetch.start()

    barrier = pltpu.get_barrier_semaphore()
    for d in range(1, n):
        pl.semaphore_signal(
            barrier, inc=1, device_id={"img": (me + d) % n}, device_id_type=MESH
        )
    for d in range(1, pn):
        pl.semaphore_signal(
            barrier, inc=1, device_id={"pose": (mine + d) % pn}, device_id_type=MESH
        )
    pl.semaphore_wait(barrier, n - 1 + pn - 1)

    square = chips == 4
    if square:
        near_x = (chip + 1 - 2 * (chip % 2)) * 2 + core
        near_y = ((chip + 2) % 4) * 2 + core
        diag = (3 - chip) * 2 + core
        first_hops = [near_x, near_y]
    else:
        first_hops = [((chip + d) % chips) * 2 + core for d in range(1, chips)]

    def own_half(h):
        return refs.at[:, h * piece : (h + 1) * piece]

    for h in range(2):
        for k, target in enumerate(first_hops):
            send(
                own_half(h), cols.at[me, h], own_send.at[k, h], gather_recv.at[me, h],
                {"img": target},
            )
        send(
            own_half(h), cols.at[me, h], own_send.at[len(first_hops), h],
            gather_recv.at[me, h], {"img": partner},
        )
    for d in range(1, n):
        send(
            seg,
            seg_all.at[pl.ds(pl.multiple_of(me * share, 8), share)],
            seg_send.at[d - 1],
            seg_recv.at[me],
            {"img": (me + d) % n},
        )
    seg_all[pl.ds(pl.multiple_of(me * share, 8), share), :] = seg[...]

    lane_sum = jnp.zeros((poses, LANES), F32)
    for g in range(depth // LANES):
        values = refs[:, g * LANES : (g + 1) * LANES].astype(F32)
        lane_noise = noise[:, pl.ds(pl.multiple_of(me * depth + g * LANES, LANES), LANES)]
        lane_sum += values * values * lane_noise
    norm_row = 0.5 * jnp.sum(lane_sum.T, axis=0, keepdims=True)
    norms[me] = jnp.broadcast_to(norm_row, (8, poses))
    for d in range(1, n):
        send(
            norms.at[me], norms.at[me], norm_send.at[d - 1], norm_recv.at[me],
            {"img": (me + d) % n},
        )

    @pl.loop(0, nblk)
    def _(b):
        at = pl.multiple_of(b * block2, block2)
        half = pl.multiple_of(b * LANES, LANES)
        re = images[:, pl.ds(at, LANES)].astype(F32)
        im = images[:, pl.ds(at + LANES, LANES)].astype(F32)
        angle = phase[:, pl.ds(half, LANES)]
        cosine = jnp.cos(angle)
        sine = jnp.sin(angle)
        real_noise = noise[:, pl.ds(at, LANES)]
        imag_noise = noise[:, pl.ds(at + LANES, LANES)]
        co_r = cosine * real_noise
        si_r = sine * real_noise
        co_i = cosine * imag_noise
        si_i = sine * imag_noise
        for t in range(trans):
            rows = pl.ds(t * count, count)
            one = slice(t, t + 1)
            weighted[rows, pl.ds(at, LANES)] = (re * co_r[one] + im * si_r[one]).astype(BF16)
            weighted[rows, pl.ds(at + LANES, LANES)] = (
                im * co_i[one] - re * si_i[one]
            ).astype(BF16)

    def multiply(block, src, h, first=False):
        start = pl.multiple_of(src * depth + h * piece, LANES)
        product = lax.dot_general(
            block,
            weighted[:, pl.ds(start, piece)],
            (((1,), (1,)), ((), ())),
            preferred_element_type=F32,
        )
        if first:
            scores[...] = product
        else:
            scores[...] += product

    def arrived(src, h):
        remote(
            own_half(h), cols.at[src, h], own_send.at[0, 0], gather_recv.at[src, h],
            {"img": partner},
        ).wait_recv()

    def hand_over(src, h, k):
        send(
            cols.at[src, h], cols.at[src, h], pass_send.at[k, h], gather_recv.at[src, h],
            {"img": partner},
        )

    def other_core(src):
        return (src // 2) * 2 + 1 - src % 2

    multiply(refs[:, 0:piece], me, 0, True)
    multiply(refs[:, piece : 2 * piece], me, 1)
    if square:
        arrived(near_x, 0)
        send(
            cols.at[near_x, 0], cols.at[near_x, 0], diag_send.at[0],
            gather_recv.at[near_x, 0], {"img": near_y},
        )
        hand_over(near_x, 0, 0)
        arrived(near_y, 0)
        hand_over(near_y, 0, 1)
        for h in range(2):
            arrived(partner, h)
            multiply(cols[partner, h], partner, h)
        multiply(cols[near_x, 0], near_x, 0)
        multiply(cols[near_y, 0], near_y, 0)
        for src in (near_x, near_y):
            arrived(other_core(src), 0)
            multiply(cols[other_core(src), 0], other_core(src), 0)
        arrived(near_y, 1)
        send(
            cols.at[near_y, 1], cols.at[near_y, 1], diag_send.at[1],
            gather_recv.at[near_y, 1], {"img": near_x},
        )
        hand_over(near_y, 1, 1)
        arrived(near_x, 1)
        hand_over(near_x, 1, 0)
        for src in (near_y, near_x):
            multiply(cols[src, 1], src, 1)
        for src in (near_y, near_x):
            arrived(other_core(src), 1)
            multiply(cols[other_core(src), 1], other_core(src), 1)
        for h in range(2):
            arrived(diag, h)
            hand_over(diag, h, 2)
        for src in (diag, other_core(diag)):
            for h in range(2):
                if src is not diag:
                    arrived(src, h)
                multiply(cols[src, h], src, h)
    else:
        for h in range(2):
            arrived(partner, h)
            multiply(cols[partner, h], partner, h)
        for k, src in enumerate(first_hops):
            for h in range(2):
                arrived(src, h)
                hand_over(src, h, k)
                multiply(cols[src, h], src, h)
                arrived(other_core(src), h)
                multiply(cols[other_core(src), h], other_core(src), h)

    norm_row = norms[me][0:1, :]
    for d in range(1, n):
        src = (me + n - d) % n
        remote(
            norms.at[src], norms.at[src], norm_send.at[0], norm_recv.at[src],
            {"img": partner},
        ).wait_recv()
        norm_row += norms[src][0:1, :]
    norm = jnp.broadcast_to(norm_row, (LANES, poses)).T
    local_peak = None
    for t in range(trans):
        value = scores[:, t * count : (t + 1) * count] - norm
        scores[:, t * count : (t + 1) * count] = value
        top = jnp.max(value, axis=0, keepdims=True)
        local_peak = top if local_peak is None else jnp.maximum(local_peak, top)
    local_sum = jnp.zeros((1, count), F32)
    for t in range(trans):
        value = jnp.exp(scores[:, t * count : (t + 1) * count] - local_peak)
        scores[:, t * count : (t + 1) * count] = value
        local_sum += jnp.sum(value, axis=0, keepdims=True)
    row = lax.broadcasted_iota(jnp.int32, (8, count), 0)
    stats[mine] = jnp.where(row == 0, local_peak, local_sum)
    for d in range(1, pn):
        send(
            stats.at[mine], stats.at[mine], stat_send.at[d - 1], stat_recv.at[mine],
            {"pose": (mine + d) % pn},
        )

    for d in range(1, n):
        src = (me + n - d) % n
        remote(
            seg,
            seg_all.at[pl.ds(pl.multiple_of(src * share, 8), share)],
            seg_send.at[0],
            seg_recv.at[src],
            {"img": partner},
        ).wait_recv()
    seg_t[...] = seg_all[...].T
    message[...] = jnp.zeros_like(message)
    for p in range(pn):
        low = ((me * pn + p) * stencils).astype(F32)
        named = seg_all[...]
        inside = jnp.where((named >= low) & (named < low + stencils), 1.0, 0.0)
        message[p, stencils : stencils + 1, 0:LANES] = jnp.sum(inside, axis=0, keepdims=True)

    for d in range(1, pn):
        src = (mine + pn - d) % pn
        remote(
            stats.at[src], stats.at[src], stat_send.at[0], stat_recv.at[src],
            {"pose": (mine + 1) % pn},
        ).wait_recv()
    peak = stats[0][0:1, :]
    for p in range(1, pn):
        peak = jnp.maximum(peak, stats[p][0:1, :])
    total = jnp.zeros((1, count), F32)
    for p in range(pn):
        total += stats[p][1:2, :] * jnp.exp(stats[p][0:1, :] - peak)
    evidence[...] = peak + jnp.log(total)
    factor = jnp.exp(local_peak - peak) / total
    for t in range(trans):
        at = slice(t * count, (t + 1) * count)
        post[:, at] = (scores[:, at] * factor).astype(BF16)

    segments = part.shape[0]
    part[...] = jnp.zeros_like(part)
    batch = 4 if nblk % 4 == 0 and segments <= 256 else 1

    @pl.loop(0, nblk // batch)
    def _(q):
        names = lax.broadcasted_iota(jnp.int32, (segments, poses), 0).astype(F32)
        rows, picks = [], []
        for u in range(batch):
            b = q * batch + u
            at = pl.multiple_of(b * block2, block2)
            sums = jnp.dot(post[...], weighted[:, pl.ds(at, block2)], preferred_element_type=F32)
            rows.append(sums.astype(BF16))
            picks.append(jnp.where(names == seg_t[pl.ds(b, 1), :], 1.0, 0.0).astype(BF16))
        part[...] += jnp.dot(
            jnp.concatenate(picks, axis=1),
            jnp.concatenate(rows, axis=0),
            preferred_element_type=F32,
        )

    part16[...] = part[...].astype(BF16)
    group = pn * stencils
    for d in range(1, n):
        target = (me + d) % n
        send(
            part16.at[pl.ds(pl.multiple_of(target * group, 16), group)],
            rows_in.at[me],
            rows_send.at[d - 1],
            rows_recv.at[me],
            {"img": target},
        )
    summed = part[pl.ds(pl.multiple_of(me * group, 16), group), :]
    for d in range(1, n):
        src = (me + n - d) % n
        remote(
            rows_in.at[src], rows_in.at[src], rows_send.at[0], rows_recv.at[src],
            {"img": partner},
        ).wait_recv()
        summed += rows_in[src].astype(F32)
    for p in range(pn):
        message[p, 0:stencils, :] = summed[p * stencils : (p + 1) * stencils, :]
    for d in range(1, pn):
        target = (mine + d) % pn
        send(
            message.at[target],
            bricks_in.at[mine],
            brick_send.at[d - 1],
            brick_recv.at[mine],
            {"pose": target},
        )
    brick = message[mine]
    fetch.wait()
    for d in range(1, pn):
        src = (mine + pn - d) % pn
        remote(
            bricks_in.at[src], bricks_in.at[src], brick_send.at[0], brick_recv.at[src],
            {"pose": (mine + 1) % pn},
        ).wait_recv()
        brick += bricks_in[src]
    gathered = brick[0:stencils, :].astype(BF16).astype(F32)
    received = jnp.sum(brick[stencils : 2 * stencils, :])
    row = lax.broadcasted_iota(jnp.int32, gathered.shape, 0)
    out = jnp.zeros((stencils, volume.shape[1]), F32)
    for s in range(stencils):
        out += jnp.dot(
            jnp.where(row == s, gathered, 0.0).astype(BF16),
            matrices[s],
            preferred_element_type=F32,
        )
    scale = lax.rsqrt(jnp.full((1, volume.shape[1]), 1.0, F32) + received)
    volume[...] = jnp.sum(out, axis=0, keepdims=True) * scale
    for copy in sends:
        copy.wait_send()


def body(images, shift_phase, noise_weight, refs, routing, stencil, interp):
    n = lax.axis_size("img")
    pn = lax.axis_size("pose")
    count, width = images.shape
    trans, pixels = shift_phase.shape
    poses, depth = refs.shape
    stencils = interp.shape[1]
    segments = n * pn * stencils
    nblk = pixels // LANES
    share = poses // n
    seg = (routing[:, 0] * stencils + stencil).astype(F32).reshape(share, nblk)
    seg = jnp.pad(seg, ((0, 0), (0, LANES - nblk)), constant_values=-1.0)
    vmem = pl.BlockSpec(memory_space=pltpu.VMEM)
    dma = pltpu.SemaphoreType.DMA
    flops = 4 * trans * count * width * poses
    volume, evidence = pl.pallas_call(
        functools.partial(kernel, n, pn),
        out_shape=(
            jax.ShapeDtypeStruct((1, interp.shape[3]), F32),
            jax.ShapeDtypeStruct((1, count), F32),
        ),
        in_specs=[vmem] * 5 + [pl.BlockSpec(memory_space=pl.ANY)],
        out_specs=(vmem, vmem),
        scratch_shapes=[
            pltpu.VMEM((n, 2, poses, depth // 2), BF16),
            pltpu.VMEM((trans * count, width), BF16),
            pltpu.VMEM((poses, trans * count), F32),
            pltpu.VMEM((poses, trans * count), BF16),
            pltpu.VMEM((poses, LANES), F32),
            pltpu.VMEM((LANES, poses), F32),
            pltpu.VMEM((n, 8, poses), F32),
            pltpu.VMEM((pn, 8, count), F32),
            pltpu.VMEM((segments, 2 * LANES), F32),
            pltpu.VMEM((segments, 2 * LANES), BF16),
            pltpu.VMEM((n, pn * stencils, 2 * LANES), BF16),
            pltpu.VMEM((pn, 2 * stencils, 2 * LANES), F32),
            pltpu.VMEM((pn, 2 * stencils, 2 * LANES), F32),
            pltpu.VMEM(interp.shape[1:], BF16),
            dma((n // 2, 2)),
            dma((n // 2, 2)),
            dma((2,)),
            dma((n, 2)),
            dma((n,)),
            dma((n,)),
            dma((n,)),
            dma((n,)),
            dma((pn,)),
            dma((pn,)),
            dma((n,)),
            dma((n,)),
            dma((pn,)),
            dma((pn,)),
            dma,
        ],
        compiler_params=pltpu.CompilerParams(
            collective_id=0, has_side_effects=True, vmem_limit_bytes=56 * 1024 * 1024
        ),
        cost_estimate=pl.CostEstimate(
            flops=flops, bytes_accessed=8 * 1024 * 1024, transcendentals=trans * count * poses
        ),
    )(images, shift_phase, noise_weight.reshape(1, width), refs, seg, interp[0])
    return (volume, evidence.reshape(count))


def solution(mesh):
    return jax.shard_map(
        body,
        mesh=mesh,
        in_specs=(
            P("img", None),
            P(),
            P(),
            P("pose", "img"),
            P(("pose", "img"), None),
            P(("pose", "img")),
            P(("img", "pose"), None, None, None),
        ),
        out_specs=(P(("img", "pose"), None), P("img")),
        check_vma=False,
    )
```

```python
import functools

import jax
import jax.numpy as jnp
from jax import lax
from jax.experimental import pallas as pl
from jax.experimental.pallas import tpu as pltpu
from jax.sharding import PartitionSpec as P

MESH = pl.DeviceIdType.MESH
F32 = jnp.float32
BF16 = jnp.bfloat16
LANES = 128


def remote(src, dst, send_sem, recv_sem, device):
    return pltpu.make_async_remote_copy(
        src_ref=src,
        dst_ref=dst,
        send_sem=send_sem,
        recv_sem=recv_sem,
        device_id=device,
        device_id_type=MESH,
    )


def kernel(
    n,
    pn,
    stencils,
    images,
    phase,
    noise,
    refs,
    routing,
    stencil,
    interp,
    volume,
    evidence,
    cols,
    weighted,
    scores,
    post,
    seg,
    seg_all,
    seg_t,
    picks,
    norms,
    stats,
    part,
    part16,
    rows_in,
    message,
    bricks_in,
    matrices,
    own_send,
    pass_send,
    diag_send,
    gather_recv,
    seg_send,
    seg_recv,
    norm_send,
    norm_recv,
    stat_send,
    stat_recv,
    rows_send,
    rows_recv,
    brick_send,
    brick_recv,
    local_sem,
):
    me = lax.axis_index("img")
    mine = lax.axis_index("pose")
    core = me % 2
    chip = me // 2
    chips = n // 2
    partner = chip * 2 + 1 - core
    count, width = images.shape
    trans = phase.shape[0]
    poses, depth = refs.shape
    piece = depth // 2
    share = seg.shape[0]
    block2 = 2 * LANES
    nblk = width // block2
    segments = part.shape[0]
    sends = []

    def send(src, dst, send_sem, recv_sem, device):
        copy = remote(src, dst, send_sem, recv_sem, device)
        copy.start()
        sends.append(copy)

    fetch = pltpu.make_async_copy(interp, matrices, local_sem)
    fetch.start()

    barrier = pltpu.get_barrier_semaphore()
    for d in range(1, n):
        pl.semaphore_signal(
            barrier, inc=1, device_id={"img": (me + d) % n}, device_id_type=MESH
        )
    for d in range(1, pn):
        pl.semaphore_signal(
            barrier, inc=1, device_id={"pose": (mine + d) % pn}, device_id_type=MESH
        )
    pl.semaphore_wait(barrier, n - 1 + pn - 1)

    square = chips == 4
    if square:
        near_x = (chip + 1 - 2 * (chip % 2)) * 2 + core
        near_y = ((chip + 2) % 4) * 2 + core
        diag = (3 - chip) * 2 + core
        first_hops = [near_x, near_y]
    else:
        first_hops = [((chip + d) % chips) * 2 + core for d in range(1, chips)]

    def own_half(h):
        return refs.at[:, h * piece : (h + 1) * piece]

    for h in range(2):
        for k, target in enumerate(first_hops):
            send(
                own_half(h), cols.at[me, h], own_send.at[k, h], gather_recv.at[me, h],
                {"img": target},
            )
        send(
            own_half(h), cols.at[me, h], own_send.at[len(first_hops), h],
            gather_recv.at[me, h], {"img": partner},
        )
    seg[...] = jnp.full(seg.shape, -1.0, F32)
    seg[:, 0:nblk] = (routing[...] * stencils + stencil[...]).astype(F32)
    for d in range(1, n):
        send(
            seg,
            seg_all.at[pl.ds(pl.multiple_of(me * share, 8), share)],
            seg_send.at[d - 1],
            seg_recv.at[me],
            {"img": (me + d) % n},
        )
    seg_all[pl.ds(pl.multiple_of(me * share, 8), share), :] = seg[...]

    lane_sum = jnp.zeros((poses, LANES), F32)
    for g in range(depth // LANES):
        values = refs[:, g * LANES : (g + 1) * LANES].astype(F32)
        lane_noise = noise[:, pl.ds(pl.multiple_of(me * depth + g * LANES, LANES), LANES)]
        lane_sum += values * values * lane_noise
    norm_row = 0.5 * jnp.sum(lane_sum.T, axis=0, keepdims=True)
    norms[me] = jnp.broadcast_to(norm_row, (8, poses))
    for d in range(1, n):
        send(
            norms.at[me], norms.at[me], norm_send.at[d - 1], norm_recv.at[me],
            {"img": (me + d) % n},
        )

    @pl.loop(0, nblk)
    def _(b):
        at = pl.multiple_of(b * block2, block2)
        half = pl.multiple_of(b * LANES, LANES)
        re = images[:, pl.ds(at, LANES)].astype(F32)
        im = images[:, pl.ds(at + LANES, LANES)].astype(F32)
        angle = phase[:, pl.ds(half, LANES)]
        cosine = jnp.cos(angle)
        sine = jnp.sin(angle)
        real_noise = noise[:, pl.ds(at, LANES)]
        imag_noise = noise[:, pl.ds(at + LANES, LANES)]
        co_r = cosine * real_noise
        si_r = sine * real_noise
        co_i = cosine * imag_noise
        si_i = sine * imag_noise
        for t in range(trans):
            rows = pl.ds(t * count, count)
            one = slice(t, t + 1)
            weighted[rows, pl.ds(at, LANES)] = (re * co_r[one] + im * si_r[one]).astype(BF16)
            weighted[rows, pl.ds(at + LANES, LANES)] = (
                im * co_i[one] - re * si_i[one]
            ).astype(BF16)

    def multiply(block, src, h, first=False):
        start = pl.multiple_of(src * depth + h * piece, LANES)
        product = lax.dot_general(
            block,
            weighted[:, pl.ds(start, piece)],
            (((1,), (1,)), ((), ())),
            preferred_element_type=F32,
        )
        if first:
            scores[...] = product
        else:
            scores[...] += product

    def arrived(src, h):
        remote(
            own_half(h), cols.at[src, h], own_send.at[0, 0], gather_recv.at[src, h],
            {"img": partner},
        ).wait_recv()

    def hand_over(src, h, k):
        send(
            cols.at[src, h], cols.at[src, h], pass_send.at[k, h], gather_recv.at[src, h],
            {"img": partner},
        )

    def other_core(src):
        return (src // 2) * 2 + 1 - src % 2

    kept = picks.shape[0]

    def choose(b):
        names = lax.broadcasted_iota(jnp.int32, (segments, poses), 0).astype(F32)
        return jnp.where(names == seg_t[pl.ds(b, 1), :], 1.0, 0.0).astype(BF16)

    def prepare():
        norm_row = norms[me][0:1, :]
        for d in range(1, n):
            src = (me + n - d) % n
            remote(
                norms.at[src], norms.at[src], norm_send.at[0], norm_recv.at[src],
                {"img": partner},
            ).wait_recv()
            norm_row += norms[src][0:1, :]
        norm = jnp.broadcast_to(norm_row, (LANES, poses)).T
        for g in range(trans * count // LANES):
            scores[:, g * LANES : (g + 1) * LANES] -= norm
        for d in range(1, n):
            src = (me + n - d) % n
            remote(
                seg,
                seg_all.at[pl.ds(pl.multiple_of(src * share, 8), share)],
                seg_send.at[0],
                seg_recv.at[src],
                {"img": partner},
            ).wait_recv()
        named = seg_all[...]
        seg_t[...] = named.T
        for p in range(pn):
            low = ((me * pn + p) * stencils).astype(F32)
            inside = jnp.where((named >= low) & (named < low + stencils), 1.0, 0.0)
            stats[mine, 8 + p : 9 + p, :] = jnp.sum(inside, axis=0, keepdims=True)
        if kept == nblk:

            @pl.loop(0, nblk)
            def _(b):
                picks[b] = choose(b)

    multiply(refs[:, 0:piece], me, 0, True)
    multiply(refs[:, piece : 2 * piece], me, 1)
    if square:
        arrived(near_x, 0)
        send(
            cols.at[near_x, 0], cols.at[near_x, 0], diag_send.at[0],
            gather_recv.at[near_x, 0], {"img": near_y},
        )
        hand_over(near_x, 0, 0)
        arrived(near_y, 0)
        hand_over(near_y, 0, 1)
        for h in range(2):
            arrived(partner, h)
            multiply(cols[partner, h], partner, h)
        multiply(cols[near_x, 0], near_x, 0)
        multiply(cols[near_y, 0], near_y, 0)
        for src in (near_x, near_y):
            arrived(other_core(src), 0)
            multiply(cols[other_core(src), 0], other_core(src), 0)
        prepare()
        arrived(near_y, 1)
        send(
            cols.at[near_y, 1], cols.at[near_y, 1], diag_send.at[1],
            gather_recv.at[near_y, 1], {"img": near_x},
        )
        hand_over(near_y, 1, 1)
        arrived(near_x, 1)
        hand_over(near_x, 1, 0)
        for src in (near_y, near_x):
            multiply(cols[src, 1], src, 1)
        for src in (near_y, near_x):
            arrived(other_core(src), 1)
            multiply(cols[other_core(src), 1], other_core(src), 1)
        for h in range(2):
            arrived(diag, h)
            hand_over(diag, h, 2)
        for src in (diag, other_core(diag)):
            for h in range(2):
                if src is not diag:
                    arrived(src, h)
                multiply(cols[src, h], src, h)
    else:
        for h in range(2):
            arrived(partner, h)
            multiply(cols[partner, h], partner, h)
        prepare()
        for k, src in enumerate(first_hops):
            for h in range(2):
                arrived(src, h)
                hand_over(src, h, k)
                multiply(cols[src, h], src, h)
                arrived(other_core(src), h)
                multiply(cols[other_core(src), h], other_core(src), h)

    local_peak = None
    for t in range(trans):
        value = scores[:, t * count : (t + 1) * count]
        top = jnp.max(value, axis=0, keepdims=True)
        local_peak = top if local_peak is None else jnp.maximum(local_peak, top)
    local_sum = jnp.zeros((1, count), F32)
    for t in range(trans):
        value = jnp.exp(scores[:, t * count : (t + 1) * count] - local_peak)
        scores[:, t * count : (t + 1) * count] = value
        local_sum += jnp.sum(value, axis=0, keepdims=True)
    row = lax.broadcasted_iota(jnp.int32, (8, count), 0)
    stats[mine, 0:8, :] = jnp.where(row == 0, local_peak, local_sum)
    for d in range(1, pn):
        send(
            stats.at[mine], stats.at[mine], stat_send.at[d - 1], stat_recv.at[mine],
            {"pose": (mine + d) % pn},
        )

    for copy in sends:
        copy.wait_send()
    sends.clear()

    for d in range(1, pn):
        src = (mine + pn - d) % pn
        remote(
            stats.at[src], stats.at[src], stat_send.at[0], stat_recv.at[src],
            {"pose": (mine + 1) % pn},
        ).wait_recv()
    peak = stats[0][0:1, :]
    for p in range(1, pn):
        peak = jnp.maximum(peak, stats[p][0:1, :])
    total = jnp.zeros((1, count), F32)
    for p in range(pn):
        total += stats[p][1:2, :] * jnp.exp(stats[p][0:1, :] - peak)
    evidence[...] = peak + jnp.log(total)
    factor = jnp.exp(local_peak - peak) / total
    for t in range(trans):
        at = slice(t * count, (t + 1) * count)
        post[:, at] = (scores[:, at] * factor).astype(BF16)

    part[...] = jnp.zeros_like(part)
    batch = 4 if nblk % 4 == 0 and kept == nblk else 1

    @pl.loop(0, nblk // batch)
    def _(q):
        rows, chosen = [], []
        for u in range(batch):
            b = q * batch + u
            at = pl.multiple_of(b * block2, block2)
            sums = jnp.dot(post[...], weighted[:, pl.ds(at, block2)], preferred_element_type=F32)
            rows.append(sums.astype(BF16))
            chosen.append(picks[b] if kept == nblk else choose(b))
        part[...] += jnp.dot(
            jnp.concatenate(chosen, axis=1),
            jnp.concatenate(rows, axis=0),
            preferred_element_type=F32,
        )

    part16[...] = part[...].astype(BF16)
    group = pn * stencils
    for d in range(1, n):
        target = (me + d) % n
        send(
            part16.at[pl.ds(pl.multiple_of(target * group, 16), group)],
            rows_in.at[me],
            rows_send.at[d - 1],
            rows_recv.at[me],
            {"img": target},
        )
    summed = part[pl.ds(pl.multiple_of(me * group, 16), group), :]
    for d in range(1, n):
        src = (me + n - d) % n
        remote(
            rows_in.at[src], rows_in.at[src], rows_send.at[0], rows_recv.at[src],
            {"img": partner},
        ).wait_recv()
        summed += rows_in[src].astype(F32)
    for p in range(pn):
        message[p] = summed[p * stencils : (p + 1) * stencils, :]
    for d in range(1, pn):
        target = (mine + d) % pn
        send(
            message.at[target],
            bricks_in.at[mine],
            brick_send.at[d - 1],
            brick_recv.at[mine],
            {"pose": target},
        )
    brick = message[mine]
    received = jnp.zeros((1, count), F32)
    for p in range(pn):
        received += stats[p, pl.ds(8 + mine, 1), :]
    received = jnp.sum(received, axis=1, keepdims=True)
    scale = lax.rsqrt(1.0 + jnp.broadcast_to(received, (1, volume.shape[1])))
    fetch.wait()
    for copy in sends:
        copy.wait_send()
    for d in range(1, pn):
        src = (mine + pn - d) % pn
        remote(
            bricks_in.at[src], bricks_in.at[src], brick_send.at[0], brick_recv.at[src],
            {"pose": (mine + 1) % pn},
        ).wait_recv()
        brick += bricks_in[src]
    row = lax.broadcasted_iota(jnp.int32, brick.shape, 0)
    spread = jnp.concatenate(
        [jnp.where(row == s, brick, 0.0).astype(BF16) for s in range(stencils)], axis=1
    )
    out = jnp.dot(spread, matrices[...], preferred_element_type=F32)
    volume[...] = jnp.sum(out, axis=0, keepdims=True) * scale


def body(images, shift_phase, noise_weight, refs, routing, stencil, interp):
    n = lax.axis_size("img")
    pn = lax.axis_size("pose")
    count, width = images.shape
    trans, pixels = shift_phase.shape
    poses, depth = refs.shape
    stencils = interp.shape[1]
    segments = n * pn * stencils
    nblk = pixels // LANES
    share = poses // n
    matrices = interp.reshape(stencils * 2 * LANES, interp.shape[3])
    kept = nblk if segments <= 256 else 1
    vmem = pl.BlockSpec(memory_space=pltpu.VMEM)
    dma = pltpu.SemaphoreType.DMA
    flops = 4 * trans * count * width * poses
    volume, evidence = pl.pallas_call(
        functools.partial(kernel, n, pn, stencils),
        out_shape=(
            jax.ShapeDtypeStruct((1, interp.shape[3]), F32),
            jax.ShapeDtypeStruct((1, count), F32),
        ),
        in_specs=[vmem] * 6 + [pl.BlockSpec(memory_space=pl.ANY)],
        out_specs=(vmem, vmem),
        scratch_shapes=[
            pltpu.VMEM((n, 2, poses, depth // 2), BF16),
            pltpu.VMEM((trans * count, width), BF16),
            pltpu.VMEM((poses, trans * count), F32),
            pltpu.VMEM((poses, trans * count), BF16),
            pltpu.VMEM((share, LANES), F32),
            pltpu.VMEM((poses, LANES), F32),
            pltpu.VMEM((LANES, poses), F32),
            pltpu.VMEM((kept, segments, poses), BF16),
            pltpu.VMEM((n, 8, poses), F32),
            pltpu.VMEM((pn, 8 + (pn + 7) // 8 * 8, count), F32),
            pltpu.VMEM((segments, 2 * LANES), F32),
            pltpu.VMEM((segments, 2 * LANES), BF16),
            pltpu.VMEM((n, pn * stencils, 2 * LANES), BF16),
            pltpu.VMEM((pn, stencils, 2 * LANES), F32),
            pltpu.VMEM((pn, stencils, 2 * LANES), F32),
            pltpu.VMEM((stencils * 2 * LANES, interp.shape[3]), BF16),
            dma((n // 2, 2)),
            dma((n // 2, 2)),
            dma((2,)),
            dma((n, 2)),
            dma((n,)),
            dma((n,)),
            dma((n,)),
            dma((n,)),
            dma((pn,)),
            dma((pn,)),
            dma((n,)),
            dma((n,)),
            dma((pn,)),
            dma((pn,)),
            dma,
        ],
        compiler_params=pltpu.CompilerParams(
            collective_id=0, has_side_effects=True, vmem_limit_bytes=46 * 1024 * 1024
        ),
        cost_estimate=pl.CostEstimate(
            flops=flops, bytes_accessed=8 * 1024 * 1024, transcendentals=trans * count * poses
        ),
    )(images, shift_phase, noise_weight.reshape(1, width), refs, routing.reshape(share, nblk), stencil.reshape(share, nblk), matrices)
    return (volume, evidence.reshape(count))


def solution(mesh):
    return jax.shard_map(
        body,
        mesh=mesh,
        in_specs=(
            P("img", None),
            P(),
            P(),
            P("pose", "img"),
            P(("pose", "img"), None),
            P(("pose", "img")),
            P(("img", "pose"), None, None, None),
        ),
        out_specs=(P(("img", "pose"), None), P("img")),
        check_vma=False,
    )
```

```python
import functools

import jax
import jax.numpy as jnp
from jax import lax
from jax.experimental import pallas as pl
from jax.experimental.pallas import tpu as pltpu
from jax.sharding import PartitionSpec as P

MESH = pl.DeviceIdType.MESH
F32 = jnp.float32
BF16 = jnp.bfloat16
LANES = 128


def remote(src, dst, send_sem, recv_sem, device):
    return pltpu.make_async_remote_copy(
        src_ref=src,
        dst_ref=dst,
        send_sem=send_sem,
        recv_sem=recv_sem,
        device_id=device,
        device_id_type=MESH,
    )


def kernel(
    n,
    pn,
    stencils,
    images,
    phase,
    noise,
    refs,
    routing,
    stencil,
    interp,
    volume,
    evidence,
    cols,
    weighted,
    scores,
    post,
    seg,
    seg_all,
    seg_t,
    picks,
    norms,
    stats,
    part,
    part16,
    rows_in,
    message,
    bricks_in,
    matrices,
    own_send,
    pass_send,
    diag_send,
    gather_recv,
    seg_send,
    seg_recv,
    norm_send,
    norm_recv,
    stat_send,
    stat_recv,
    rows_send,
    rows_recv,
    brick_send,
    brick_recv,
    local_sem,
):
    me = lax.axis_index("img")
    mine = lax.axis_index("pose")
    core = me % 2
    chip = me // 2
    chips = n // 2
    partner = chip * 2 + 1 - core
    count, width = images.shape
    trans = phase.shape[0]
    poses, depth = refs.shape
    piece = depth // 2
    share = seg.shape[0]
    block2 = 2 * LANES
    nblk = width // block2
    segments = part.shape[0]
    sends = []

    def send(src, dst, send_sem, recv_sem, device):
        copy = remote(src, dst, send_sem, recv_sem, device)
        copy.start()
        sends.append(copy)

    fetch = pltpu.make_async_copy(interp, matrices, local_sem)
    fetch.start()

    barrier = pltpu.get_barrier_semaphore()
    for d in range(1, n):
        pl.semaphore_signal(
            barrier, inc=1, device_id={"img": (me + d) % n}, device_id_type=MESH
        )
    for d in range(1, pn):
        pl.semaphore_signal(
            barrier, inc=1, device_id={"pose": (mine + d) % pn}, device_id_type=MESH
        )
    pl.semaphore_wait(barrier, n - 1 + pn - 1)

    square = chips == 4
    if square:
        near_x = (chip + 1 - 2 * (chip % 2)) * 2 + core
        near_y = ((chip + 2) % 4) * 2 + core
        diag = (3 - chip) * 2 + core
        first_hops = [near_x, near_y]
    else:
        first_hops = [((chip + d) % chips) * 2 + core for d in range(1, chips)]

    def own_half(h):
        return refs.at[:, h * piece : (h + 1) * piece]

    for h in range(2):
        for k, target in enumerate(first_hops):
            send(
                own_half(h), cols.at[me, h], own_send.at[k, h], gather_recv.at[me, h],
                {"img": target},
            )
        send(
            own_half(h), cols.at[me, h], own_send.at[len(first_hops), h],
            gather_recv.at[me, h], {"img": partner},
        )
    seg[...] = jnp.full(seg.shape, -1.0, F32)
    seg[:, 0:nblk] = (routing[...] * stencils + stencil[...]).astype(F32)
    for d in range(1, n):
        send(
            seg,
            seg_all.at[pl.ds(pl.multiple_of(me * share, 8), share)],
            seg_send.at[d - 1],
            seg_recv.at[me],
            {"img": (me + d) % n},
        )
    seg_all[pl.ds(pl.multiple_of(me * share, 8), share), :] = seg[...]

    lane_sum = jnp.zeros((poses, LANES), F32)
    for g in range(depth // LANES):
        values = refs[:, g * LANES : (g + 1) * LANES].astype(F32)
        lane_noise = noise[:, pl.ds(pl.multiple_of(me * depth + g * LANES, LANES), LANES)]
        lane_sum += values * values * lane_noise
    norm_row = 0.5 * jnp.sum(lane_sum.T, axis=0, keepdims=True)
    norms[me] = jnp.broadcast_to(norm_row, (8, poses))
    for d in range(1, n):
        send(
            norms.at[me], norms.at[me], norm_send.at[d - 1], norm_recv.at[me],
            {"img": (me + d) % n},
        )

    @pl.loop(0, nblk)
    def _(b):
        at = pl.multiple_of(b * block2, block2)
        half = pl.multiple_of(b * LANES, LANES)
        re = images[:, pl.ds(at, LANES)].astype(F32)
        im = images[:, pl.ds(at + LANES, LANES)].astype(F32)
        angle = phase[:, pl.ds(half, LANES)]
        cosine = jnp.cos(angle)
        sine = jnp.sin(angle)
        real_noise = noise[:, pl.ds(at, LANES)]
        imag_noise = noise[:, pl.ds(at + LANES, LANES)]
        co_r = cosine * real_noise
        si_r = sine * real_noise
        co_i = cosine * imag_noise
        si_i = sine * imag_noise
        for t in range(trans):
            rows = pl.ds(t * count, count)
            one = slice(t, t + 1)
            weighted[rows, pl.ds(at, LANES)] = (re * co_r[one] + im * si_r[one]).astype(BF16)
            weighted[rows, pl.ds(at + LANES, LANES)] = (
                im * co_i[one] - re * si_i[one]
            ).astype(BF16)

    def multiply(block, src, h, first=False):
        start = pl.multiple_of(src * depth + h * piece, LANES)
        product = lax.dot_general(
            block,
            weighted[:, pl.ds(start, piece)],
            (((1,), (1,)), ((), ())),
            preferred_element_type=F32,
        )
        if first:
            scores[...] = product
        else:
            scores[...] += product

    def arrived(src, h):
        remote(
            own_half(h), cols.at[src, h], own_send.at[0, 0], gather_recv.at[src, h],
            {"img": partner},
        ).wait_recv()

    def hand_over(src, h, k):
        send(
            cols.at[src, h], cols.at[src, h], pass_send.at[k, h], gather_recv.at[src, h],
            {"img": partner},
        )

    def other_core(src):
        return (src // 2) * 2 + 1 - src % 2

    kept = picks.shape[0]

    def choose(b):
        names = lax.broadcasted_iota(jnp.int32, (segments, poses), 0).astype(F32)
        return jnp.where(names == seg_t[pl.ds(b, 1), :], 1.0, 0.0).astype(BF16)

    def prepare():
        norm_row = norms[me][0:1, :]
        for d in range(1, n):
            src = (me + n - d) % n
            remote(
                norms.at[src], norms.at[src], norm_send.at[0], norm_recv.at[src],
                {"img": partner},
            ).wait_recv()
            norm_row += norms[src][0:1, :]
        norm = jnp.broadcast_to(norm_row, (LANES, poses)).T
        for g in range(trans * count // LANES):
            scores[:, g * LANES : (g + 1) * LANES] -= norm
        for d in range(1, n):
            src = (me + n - d) % n
            remote(
                seg,
                seg_all.at[pl.ds(pl.multiple_of(src * share, 8), share)],
                seg_send.at[0],
                seg_recv.at[src],
                {"img": partner},
            ).wait_recv()
        named = seg_all[...]
        seg_t[...] = named.T
        for p in range(pn):
            low = ((me * pn + p) * stencils).astype(F32)
            inside = jnp.where((named >= low) & (named < low + stencils), 1.0, 0.0)
            stats[mine, 8 + p : 9 + p, :] = jnp.sum(inside, axis=0, keepdims=True)
        if kept == nblk:

            @pl.loop(0, nblk)
            def _(b):
                picks[b] = choose(b)

    multiply(refs[:, 0:piece], me, 0, True)
    multiply(refs[:, piece : 2 * piece], me, 1)
    if square:
        arrived(near_x, 0)
        send(
            cols.at[near_x, 0], cols.at[near_x, 0], diag_send.at[0],
            gather_recv.at[near_x, 0], {"img": near_y},
        )
        hand_over(near_x, 0, 0)
        arrived(near_y, 0)
        hand_over(near_y, 0, 1)
        for h in range(2):
            arrived(partner, h)
            multiply(cols[partner, h], partner, h)
        multiply(cols[near_x, 0], near_x, 0)
        multiply(cols[near_y, 0], near_y, 0)
        arrived(near_y, 1)
        send(
            cols.at[near_y, 1], cols.at[near_y, 1], diag_send.at[1],
            gather_recv.at[near_y, 1], {"img": near_x},
        )
        hand_over(near_y, 1, 1)
        arrived(near_x, 1)
        hand_over(near_x, 1, 0)
        for src in (near_x, near_y):
            arrived(other_core(src), 0)
            multiply(cols[other_core(src), 0], other_core(src), 0)
        for src in (near_y, near_x):
            multiply(cols[src, 1], src, 1)
        for src in (near_y, near_x):
            arrived(other_core(src), 1)
            multiply(cols[other_core(src), 1], other_core(src), 1)
        prepare()
        for h in range(2):
            arrived(diag, h)
            hand_over(diag, h, 2)
        for src in (diag, other_core(diag)):
            for h in range(2):
                if src is not diag:
                    arrived(src, h)
                multiply(cols[src, h], src, h)
    else:
        for h in range(2):
            arrived(partner, h)
            multiply(cols[partner, h], partner, h)
        prepare()
        for k, src in enumerate(first_hops):
            for h in range(2):
                arrived(src, h)
                hand_over(src, h, k)
                multiply(cols[src, h], src, h)
                arrived(other_core(src), h)
                multiply(cols[other_core(src), h], other_core(src), h)

    local_peak = None
    for t in range(trans):
        value = scores[:, t * count : (t + 1) * count]
        top = jnp.max(value, axis=0, keepdims=True)
        local_peak = top if local_peak is None else jnp.maximum(local_peak, top)
    local_sum = jnp.zeros((1, count), F32)
    for t in range(trans):
        value = jnp.exp(scores[:, t * count : (t + 1) * count] - local_peak)
        scores[:, t * count : (t + 1) * count] = value
        local_sum += jnp.sum(value, axis=0, keepdims=True)
    row = lax.broadcasted_iota(jnp.int32, (8, count), 0)
    stats[mine, 0:8, :] = jnp.where(row == 0, local_peak, local_sum)
    for d in range(1, pn):
        send(
            stats.at[mine], stats.at[mine], stat_send.at[d - 1], stat_recv.at[mine],
            {"pose": (mine + d) % pn},
        )

    for copy in sends:
        copy.wait_send()
    sends.clear()

    for d in range(1, pn):
        src = (mine + pn - d) % pn
        remote(
            stats.at[src], stats.at[src], stat_send.at[0], stat_recv.at[src],
            {"pose": (mine + 1) % pn},
        ).wait_recv()
    peak = stats[0][0:1, :]
    for p in range(1, pn):
        peak = jnp.maximum(peak, stats[p][0:1, :])
    total = jnp.zeros((1, count), F32)
    for p in range(pn):
        total += stats[p][1:2, :] * jnp.exp(stats[p][0:1, :] - peak)
    evidence[...] = peak + jnp.log(total)
    factor = jnp.exp(local_peak - peak) / total
    for t in range(trans):
        at = slice(t * count, (t + 1) * count)
        post[:, at] = (scores[:, at] * factor).astype(BF16)

    part[...] = jnp.zeros_like(part)
    batch = 4 if nblk % 4 == 0 and kept == nblk else 1

    @pl.loop(0, nblk // batch)
    def _(q):
        rows, chosen = [], []
        for u in range(batch):
            b = q * batch + u
            at = pl.multiple_of(b * block2, block2)
            sums = jnp.dot(post[...], weighted[:, pl.ds(at, block2)], preferred_element_type=F32)
            rows.append(sums.astype(BF16))
            chosen.append(picks[b] if kept == nblk else choose(b))
        part[...] += jnp.dot(
            jnp.concatenate(chosen, axis=1),
            jnp.concatenate(rows, axis=0),
            preferred_element_type=F32,
        )

    part16[...] = part[...].astype(BF16)
    group = pn * stencils
    for d in range(1, n):
        target = (me + d) % n
        send(
            part16.at[pl.ds(pl.multiple_of(target * group, 16), group)],
            rows_in.at[me],
            rows_send.at[d - 1],
            rows_recv.at[me],
            {"img": target},
        )
    summed = part[pl.ds(pl.multiple_of(me * group, 16), group), :]
    for d in range(1, n):
        src = (me + n - d) % n
        remote(
            rows_in.at[src], rows_in.at[src], rows_send.at[0], rows_recv.at[src],
            {"img": partner},
        ).wait_recv()
        summed += rows_in[src].astype(F32)
    for p in range(pn):
        message[p] = summed[p * stencils : (p + 1) * stencils, :]
    for d in range(1, pn):
        target = (mine + d) % pn
        send(
            message.at[target],
            bricks_in.at[mine],
            brick_send.at[d - 1],
            brick_recv.at[mine],
            {"pose": target},
        )
    brick = message[mine]
    received = jnp.zeros((1, count), F32)
    for p in range(pn):
        received += stats[p, pl.ds(8 + mine, 1), :]
    received = jnp.sum(received, axis=1, keepdims=True)
    scale = lax.rsqrt(1.0 + jnp.broadcast_to(received, (1, volume.shape[1])))
    fetch.wait()
    for copy in sends:
        copy.wait_send()
    for d in range(1, pn):
        src = (mine + pn - d) % pn
        remote(
            bricks_in.at[src], bricks_in.at[src], brick_send.at[0], brick_recv.at[src],
            {"pose": (mine + 1) % pn},
        ).wait_recv()
        brick += bricks_in[src]
    row = lax.broadcasted_iota(jnp.int32, brick.shape, 0)
    spread = jnp.concatenate(
        [jnp.where(row == s, brick, 0.0).astype(BF16) for s in range(stencils)], axis=1
    )
    out = jnp.dot(spread, matrices[...], preferred_element_type=F32)
    volume[...] = jnp.sum(out, axis=0, keepdims=True) * scale


def body(images, shift_phase, noise_weight, refs, routing, stencil, interp):
    n = lax.axis_size("img")
    pn = lax.axis_size("pose")
    count, width = images.shape
    trans, pixels = shift_phase.shape
    poses, depth = refs.shape
    stencils = interp.shape[1]
    segments = n * pn * stencils
    nblk = pixels // LANES
    share = poses // n
    matrices = interp.reshape(stencils * 2 * LANES, interp.shape[3])
    kept = nblk if segments <= 256 else 1
    vmem = pl.BlockSpec(memory_space=pltpu.VMEM)
    dma = pltpu.SemaphoreType.DMA
    flops = 4 * trans * count * width * poses
    volume, evidence = pl.pallas_call(
        functools.partial(kernel, n, pn, stencils),
        out_shape=(
            jax.ShapeDtypeStruct((1, interp.shape[3]), F32),
            jax.ShapeDtypeStruct((1, count), F32),
        ),
        in_specs=[vmem] * 6 + [pl.BlockSpec(memory_space=pl.ANY)],
        out_specs=(vmem, vmem),
        scratch_shapes=[
            pltpu.VMEM((n, 2, poses, depth // 2), BF16),
            pltpu.VMEM((trans * count, width), BF16),
            pltpu.VMEM((poses, trans * count), F32),
            pltpu.VMEM((poses, trans * count), BF16),
            pltpu.VMEM((share, LANES), F32),
            pltpu.VMEM((poses, LANES), F32),
            pltpu.VMEM((LANES, poses), F32),
            pltpu.VMEM((kept, segments, poses), BF16),
            pltpu.VMEM((n, 8, poses), F32),
            pltpu.VMEM((pn, 8 + (pn + 7) // 8 * 8, count), F32),
            pltpu.VMEM((segments, 2 * LANES), F32),
            pltpu.VMEM((segments, 2 * LANES), BF16),
            pltpu.VMEM((n, pn * stencils, 2 * LANES), BF16),
            pltpu.VMEM((pn, stencils, 2 * LANES), F32),
            pltpu.VMEM((pn, stencils, 2 * LANES), F32),
            pltpu.VMEM((stencils * 2 * LANES, interp.shape[3]), BF16),
            dma((n // 2, 2)),
            dma((n // 2, 2)),
            dma((2,)),
            dma((n, 2)),
            dma((n,)),
            dma((n,)),
            dma((n,)),
            dma((n,)),
            dma((pn,)),
            dma((pn,)),
            dma((n,)),
            dma((n,)),
            dma((pn,)),
            dma((pn,)),
            dma,
        ],
        compiler_params=pltpu.CompilerParams(
            collective_id=0, has_side_effects=True, vmem_limit_bytes=56 * 1024 * 1024
        ),
        cost_estimate=pl.CostEstimate(
            flops=flops, bytes_accessed=8 * 1024 * 1024, transcendentals=trans * count * poses
        ),
    )(images, shift_phase, noise_weight.reshape(1, width), refs, routing.reshape(share, nblk), stencil.reshape(share, nblk), matrices)
    return (volume, evidence.reshape(count))


def solution(mesh):
    return jax.shard_map(
        body,
        mesh=mesh,
        in_specs=(
            P("img", None),
            P(),
            P(),
            P("pose", "img"),
            P(("pose", "img"), None),
            P(("pose", "img")),
            P(("img", "pose"), None, None, None),
        ),
        out_specs=(P(("img", "pose"), None), P("img")),
        check_vma=False,
    )
```
